256 devices in a mesh: grp: 2 (over core), seq: 16 (over x, y), row: 8 (over z).
Axes of the slice: x: 4, y: 4, z: 8, core: 2. Of those that a mesh axis runs over, the one named last changes fastest.
Arguments:
- latent_pool: bfloat16 [2, 2048, 64, 576], P('grp', ('seq', 'row')), may hold values from -24 to 24
- block_table: int32 [2, 128, 16, 1], P('grp', ('seq', 'row')), may hold values from 0 to 15, as said below
- lengths: int32 [2, 16], replicated, may hold values from 1024 to 8192
- row_request: int32 [2, 16], P('grp'), may hold values from 0 to 15, each once within a row
- queries: bfloat16 [2, 16, 4, 128, 192], P('grp', 'row', None, 'seq'), may hold values from -24 to 24
- new_latent: bfloat16 [2, 16, 4, 576], P('grp', 'row'), may hold values from -6 to 6
- w_uk: bfloat16 [128, 128, 512], P('seq'), may hold values from -0.5 to 0.5
- w_uv: bfloat16 [128, 512, 128], P('seq'), may hold values from -0.25 to 0.25
Outputs:
- attn_out: bfloat16 [2, 16, 4, 128, 128], P('grp', 'row', None, 'seq')
The draws below stay inside these ranges and needn't reach their ends.
Inputs may be any that keep to these rules, and one draw needn't show every extreme that they name: Each block block_table[g, d] holds every page number of 0 to 15 once. row_request[g] is a permutation of the 16 requests.
All inputs are finite; a program needn't handle non-finite values.
Results may differ from the reference program's by a relative error of at most 0.02.
Values may be sent and summed in bfloat16 or wider, within the bound.
No kernel may reach another device: no remote copies, remote signals or barrier semaphores. Data moves between devices by JAX's collectives and lax.ppermute only.
A program may use at most 64 MiB of HBM per device.

```python
import jax
import jax.numpy as jnp
from jax import lax

HEADS = 128
KVL = 512
ROPE = 64
NOPE = 128
VH = 128
NEW = 4
PAGE = 64
LEN = 8192
REQS = 16
NBLK = 128
BPD = 1
POOL = 16


def draw_latent_pool(key, part):
    key = jax.random.fold_in(key, 3)
    full_shape = (2, NBLK * POOL, PAGE, KVL + ROPE)
    values = jnp.clip(jax.random.normal(key, full_shape, jnp.float32), -6.0, 6.0)
    return values.astype(jnp.bfloat16)


def draw_queries(key, part):
    key = jax.random.fold_in(key, 5)
    full_shape = (2, REQS, NEW, HEADS, NOPE + ROPE)
    values = jnp.clip(jax.random.normal(key, full_shape, jnp.float32), -6.0, 6.0)
    return values.astype(jnp.bfloat16)


def draw_block_table(key, part):
    key = jax.random.fold_in(key, 7)
    page_keys = jax.random.split(key, 2 * NBLK)
    orders = jax.vmap(lambda one_key: jax.random.permutation(one_key, POOL))(page_keys)
    return orders.reshape(2, NBLK, REQS, BPD).astype(jnp.int32)


def draw_lengths(key, part):
    key = jax.random.fold_in(key, 11)
    shortest = LEN // 8
    values = jax.random.randint(key, (2, REQS), shortest, LEN + 1)
    first_slot = jax.random.randint(jax.random.fold_in(key, 1), (2,), 0, REQS)
    step_gap = jax.random.randint(jax.random.fold_in(key, 2), (2,), 1, REQS)
    second_slot = (first_slot + step_gap) % REQS
    groups = jnp.arange(2)
    values = values.at[groups, first_slot].set(LEN)
    values = values.at[groups, second_slot].set(shortest)
    return values.astype(jnp.int32)


def levels(own_key, dims, cuts, least, largest):
    level = 1.0
    for position, blocks in cuts:
        draws = jax.random.uniform(jax.random.fold_in(jax.random.fold_in(own_key, 6), position), (blocks,), jnp.float32, least / len(cuts), largest / len(cuts))
        level = level * jnp.repeat(jnp.exp(draws), dims[position] // blocks).reshape((-1,) + (1,) * (len(dims) - 1 - position))
    return level


def noise(key, dims, spread, limit, cuts=(), held_as=jnp.bfloat16):
    values = jax.random.normal(key, dims, jnp.float32) * spread
    if len(cuts) > 0:
        values = levels(key, dims, cuts, -0.22, 0.18) * values
    return jnp.clip(values, min=-limit, max=limit).astype(held_as)


def setup_inputs(seed: int = 0) -> dict:
    streams_of = jax.random.split(jax.random.key(seed), 9)
    return {
        "latent_pool": draw_latent_pool(jax.random.fold_in(streams_of[8], 71), 0),
        "block_table": draw_block_table(jax.random.fold_in(streams_of[8], 71), 0),
        "lengths": draw_lengths(jax.random.fold_in(streams_of[8], 71), 0),
        "row_request": jax.vmap(lambda own: jax.random.permutation(own, REQS))(jax.random.split(streams_of[3], 2)).reshape((2, REQS)).astype(jnp.int32),
        "queries": draw_queries(jax.random.fold_in(streams_of[8], 71), 0),
        "new_latent": noise(streams_of[5], (2, REQS, NEW, KVL + ROPE), 1.0, 6.0, ((0, 2), (1, 8))),
        "w_uk": noise(streams_of[6], (HEADS, NOPE, KVL), NOPE ** -0.5, 0.5, ((0, 16),)),
        "w_uv": noise(streams_of[7], (HEADS, KVL, VH), KVL ** -0.5, 0.25, ((0, 16),)),
    }


def row_output(pool_blocks, table_blocks, batch_len, request, query_raw, latent_new, w_key, w_value):
    gathered = jax.vmap(lambda pool_block, table_block: pool_block[table_block])(pool_blocks, table_blocks[:, request, :])
    prompt_cache = gathered.reshape(LEN, KVL + ROPE)
    q_lat = jnp.einsum("nhk,hkc->nhc", query_raw[:, :, :NOPE].astype(jnp.float32), w_key).astype(jnp.bfloat16)
    query_full = jnp.concatenate([q_lat, query_raw[:, :, NOPE:]], axis=-1)
    query_full = lax.optimization_barrier(query_full).astype(jnp.float32)
    all_keys = jnp.concatenate([prompt_cache, latent_new], axis=0).astype(jnp.float32)
    scores = jnp.einsum("nhc,kc->nhk", query_full, all_keys) * ((NOPE + ROPE) ** -0.5)
    positions = jnp.arange(LEN, dtype=jnp.int32)
    in_prompt = jnp.broadcast_to((positions < batch_len[request])[None, :], (NEW, LEN))
    new_steps = jnp.arange(NEW, dtype=jnp.int32)
    earlier = new_steps[None, :] <= new_steps[:, None]
    visible = jnp.concatenate([in_prompt, earlier], axis=1)[:, None, :]
    best_score = jnp.max(jnp.where(visible, scores, -jnp.inf), axis=-1, keepdims=True)
    weights = jnp.where(visible, jnp.exp(scores - best_score), 0.0)
    weight_sum = jnp.sum(weights, axis=-1, keepdims=True)
    rounded = lax.optimization_barrier(weights.astype(jnp.bfloat16)).astype(jnp.float32)
    latent_out = (jnp.einsum("nhk,kc->nhc", rounded, all_keys[:, :KVL]) / weight_sum).astype(jnp.bfloat16)
    latent_out = lax.optimization_barrier(latent_out).astype(jnp.float32)
    return jnp.einsum("nhc,hcv->nhv", latent_out, w_value).astype(jnp.bfloat16)


def reference(latent_pool, block_table, lengths, row_request, queries, new_latent, w_uk, w_uv):
    w_key = w_uk.astype(jnp.float32)
    w_value = w_uv.astype(jnp.float32)
    pool_groups = latent_pool.reshape(2, NBLK, POOL, PAGE, KVL + ROPE)
    outputs = []
    for group_id in range(2):
        source = 1 - group_id

        def one_row(row_id, group_id=group_id, source=source):
            return row_output(pool_groups[source], block_table[source], lengths[source],
                              row_request[group_id, row_id], queries[group_id, row_id],
                              new_latent[group_id, row_id], w_key, w_value)

        outputs.append(lax.map(one_row, jnp.arange(REQS, dtype=jnp.int32)))
    return jnp.stack(outputs, axis=0)
```

```python
import functools

import jax
import jax.numpy as jnp
from jax import lax
from jax.experimental import pallas as pl
from jax.experimental.pallas import tpu as pltpu
from jax.sharding import PartitionSpec as P

FILL_LOW = -1e30
LANES = 128
FOLD = 16
PARTS = 8
NT = (((1,), (1,)), ((), ()))


def smem():
    return pl.BlockSpec(memory_space=pltpu.SMEM)


def vmem():
    return pl.BlockSpec(memory_space=pltpu.VMEM)


def params(mib):
    return pltpu.CompilerParams(vmem_limit_bytes=mib << 20)


def pack_kernel(request_ref, table_ref, pool_ref, out_ref):
    n_row = out_ref.shape[0]
    rows_dev = request_ref.shape[1] // n_row
    latent = (out_ref.shape[2] - LANES) // rows_dev
    for peer in range(n_row):
        ropes = []
        for r in range(rows_dev):
            page = table_ref[0, request_ref[0, peer * rows_dev + r]]
            out_ref[peer, :, r * latent : (r + 1) * latent] = pool_ref[page, :, :latent]
            ropes.append(pool_ref[page, :, latent:])
        out_ref[peer, :, rows_dev * latent :] = jnp.concatenate(ropes, axis=1)


def query_kernel(query_ref, w_ref, out_ref):
    heads, nope, latent = w_ref.shape
    rows = query_ref.shape[0]
    plain = query_ref[:, :nope]
    head_of = lax.broadcasted_iota(jnp.int32, (rows, latent), 0) % heads
    total = jnp.zeros((rows, latent), jnp.float32)
    for h in range(heads):
        one = jnp.dot(plain, w_ref[h], preferred_element_type=jnp.float32)
        total = jnp.where(head_of == h, one, total)
    out_ref[:, :latent] = total.astype(jnp.bfloat16)
    rope = query_ref[:, nope:].astype(jnp.float32)
    second = lax.broadcasted_iota(jnp.int32, rope.shape, 0) >= rows // 2
    zero = jnp.zeros_like(rope)
    both = jnp.concatenate([jnp.where(second, zero, rope), jnp.where(second, rope, zero)], axis=1)
    out_ref[:, latent:] = both.astype(jnp.bfloat16)


def split_bf16(value, count):
    parts = []
    for _ in range(count):
        part = value.astype(jnp.bfloat16).astype(jnp.float32)
        parts.append(part)
        value = value - part
    return parts


def attend_kernel(scale, place_ref, lengths_ref, request_ref, cache_ref, *refs):
    query_refs, out_ref = refs[:-1], refs[-1]
    group, seq, row = place_ref[0], place_ref[1], place_ref[2]
    n_seq = out_ref.shape[0]
    keys = cache_ref.shape[0]
    blocks_each = n_seq // len(query_refs)
    block_rows = query_refs[0].shape[0] // blocks_each
    rows_dev = 2
    half = block_rows // rows_dev
    latent = (cache_ref.shape[1] - LANES) // rows_dev
    rows = n_seq * half
    ropes = cache_ref[:, rows_dev * latent :]
    position = lax.broadcasted_iota(jnp.int32, (1, keys), 1) + seq * keys
    lane = lax.broadcasted_iota(jnp.int32, (rows, LANES), 1)
    inner = lax.broadcasted_iota(jnp.int32, (rows, LANES), 0) % half
    folded = None
    for r in range(rows_dev):
        length = lengths_ref[group, request_ref[0, row * rows_dev + r]]
        visible = position < length
        cache = cache_ref[:, r * latent : (r + 1) * latent]
        query = jnp.concatenate(
            [
                query_ref[b * block_rows + r * half : b * block_rows + (r + 1) * half, :]
                for query_ref in query_refs
                for b in range(blocks_each)
            ],
            axis=0,
        )
        scores = lax.dot_general(query[:, :latent], cache, NT, preferred_element_type=jnp.float32)
        scores += lax.dot_general(query[:, latent:], ropes, NT, preferred_element_type=jnp.float32)
        scores = jnp.where(visible, scores * scale, FILL_LOW)
        best = jnp.max(scores, axis=1, keepdims=True)
        weights = jnp.where(visible, jnp.exp(scores - best), 0.0)
        weight_sum = jnp.sum(weights, axis=1, keepdims=True)
        value = jnp.dot(
            weights.astype(jnp.bfloat16), cache, preferred_element_type=jnp.float32
        ).astype(jnp.bfloat16)
        base = PARTS * (r * (half // FOLD) + inner // FOLD)
        stats = jnp.zeros((rows, LANES), jnp.float32)
        for j, part in enumerate(split_bf16(best, 3) + split_bf16(weight_sum, 2)):
            stats = jnp.where(lane == base + j, part, stats)
        stats = jnp.sum(stats.reshape(n_seq, half // FOLD, FOLD, LANES), axis=1)
        folded = stats if folded is None else folded + stats
        for b in range(n_seq):
            for c in range(latent // LANES):
                out_ref[seq ^ b, c * block_rows + r * half : c * block_rows + (r + 1) * half, :] = (
                    value[b * half : (b + 1) * half, c * LANES : (c + 1) * LANES]
                )
    tail = (latent // LANES) * block_rows
    for b in range(n_seq):
        out_ref[seq ^ b, tail:, :] = folded[b].astype(jnp.bfloat16)


def merge_kernel(scale, got_ref, query_ref, new_ref, w_ref, out_ref):
    n_seq = got_ref.shape[0]
    heads, latent, _ = w_ref.shape
    rows = query_ref.shape[0]
    chunks = latent // LANES
    tail = chunks * rows
    row_id = lax.broadcasted_iota(jnp.int32, (rows, LANES), 0)
    lane = lax.broadcasted_iota(jnp.int32, (rows, LANES), 1)
    base = PARTS * (row_id // FOLD)
    in_best = (lane >= base) & (lane < base + 3)
    in_sum = (lane >= base + 3) & (lane < base + 5)
    bests, sums = [], []
    for i in range(n_seq):
        stats = got_ref[i, tail:, :].astype(jnp.float32)
        stats = jnp.concatenate([stats] * (rows // FOLD), axis=0)
        bests.append(jnp.sum(jnp.where(in_best, stats, 0.0), axis=1, keepdims=True))
        sums.append(jnp.sum(jnp.where(in_sum, stats, 0.0), axis=1, keepdims=True))
    new_keys = new_ref[...].astype(jnp.float32)
    count = new_keys.shape[0]
    steps = count // 2
    new_lat = new_keys[:, :latent]
    rope = new_keys[:, latent:]
    second = lax.broadcasted_iota(jnp.int32, rope.shape, 0) >= steps
    zero = jnp.zeros_like(rope)
    new_rope = jnp.concatenate([jnp.where(second, zero, rope), jnp.where(second, rope, zero)], axis=1)
    new_scores = lax.dot_general(
        query_ref[:, :latent], new_lat.astype(jnp.bfloat16), NT, preferred_element_type=jnp.float32
    ) + lax.dot_general(
        query_ref[:, latent:], new_rope.astype(jnp.bfloat16), NT, preferred_element_type=jnp.float32
    )
    query_id = lax.broadcasted_iota(jnp.int32, (rows, count), 0)
    key_id = lax.broadcasted_iota(jnp.int32, (rows, count), 1)
    half = rows // 2
    causal = (query_id // half == key_id // steps) & (
        key_id % steps <= (query_id % half) // heads
    )
    new_scores = jnp.where(causal, new_scores * scale, FILL_LOW)
    best = jnp.max(new_scores, axis=1, keepdims=True)
    for one in bests:
        best = jnp.maximum(best, one)
    new_weights = jnp.where(causal, jnp.exp(new_scores - best), 0.0)
    total = jnp.sum(new_weights, axis=1, keepdims=True)
    new_weights = new_weights.astype(jnp.bfloat16).astype(jnp.float32)
    factors = [jnp.exp(one - best) for one in bests]
    for factor, one in zip(factors, sums):
        total = total + factor * one
    pieces = []
    for c in range(chunks):
        value = jnp.zeros((rows, LANES), jnp.float32)
        for j in range(count):
            value = value + new_weights[:, j : j + 1] * new_lat[j : j + 1, c * LANES : (c + 1) * LANES]
        for i in range(n_seq):
            value = value + factors[i] * got_ref[i, c * rows : (c + 1) * rows, :].astype(jnp.float32)
        pieces.append((value / total).astype(jnp.bfloat16))
    latent_out = jnp.concatenate(pieces, axis=1)
    head_of = lax.broadcasted_iota(jnp.int32, out_ref.shape, 0) % heads
    result = jnp.zeros(out_ref.shape, jnp.float32)
    for h in range(heads):
        one = jnp.dot(latent_out, w_ref[h], preferred_element_type=jnp.float32)
        result = jnp.where(head_of == h, one, result)
    out_ref[...] = result.astype(jnp.bfloat16)


def per_device(latent_pool, block_table, lengths, row_request, queries, new_latent, w_uk, w_uv):
    n_seq = lax.axis_size("seq")
    n_row = lax.axis_size("row")
    n_near = 4
    group = lax.axis_index("grp")
    _, rows_dev, n_new, head_dev, query_width = queries.shape
    _, page_rows, lat_width = latent_pool.shape[1:]
    latent_dim = w_uk.shape[2]
    value_dim = w_uv.shape[2]
    block_rows = rows_dev * n_new * head_dev
    scale = query_width ** (-0.5)
    swap = [(0, 1), (1, 0)]
    bf16 = jnp.bfloat16

    request = lax.ppermute(row_request, "grp", swap)
    new_keys = lax.ppermute(new_latent.reshape(rows_dev * n_new, lat_width), "grp", swap)
    packed = pl.pallas_call(
        pack_kernel,
        out_shape=jax.ShapeDtypeStruct((n_row, page_rows, rows_dev * latent_dim + LANES), bf16),
        in_specs=[smem(), smem(), vmem()],
        out_specs=vmem(),
        compiler_params=params(16),
        name="pack",
    )(request, block_table.reshape(1, -1), latent_pool[0])
    got_cache = lax.all_to_all(packed, "row", 0, 0, tiled=True)

    own_query = pl.pallas_call(
        query_kernel,
        out_shape=jax.ShapeDtypeStruct((block_rows, latent_dim + LANES), bf16),
        in_specs=[vmem(), vmem()],
        out_specs=vmem(),
        compiler_params=params(16),
        name="query",
    )(queries.reshape(block_rows, query_width), w_uk)
    near = []
    for k in range(n_near):
        route = [
            (g * n_seq + s, (1 - g) * n_seq + (s ^ k)) for g in range(2) for s in range(n_seq)
        ]
        near.append(lax.ppermute(own_query, ("grp", "seq"), route))
    near_query = jnp.concatenate(near, axis=0)
    all_query = [near_query]
    for j in range(1, n_seq // n_near):
        route = [(s, s ^ (j * n_near)) for s in range(n_seq)]
        all_query.append(lax.ppermute(near_query, "seq", route))

    place = jnp.stack([group, lax.axis_index("seq"), lax.axis_index("row")]).astype(jnp.int32)
    message = pl.pallas_call(
        functools.partial(attend_kernel, scale),
        out_shape=jax.ShapeDtypeStruct(
            (n_seq, block_rows * latent_dim // LANES + FOLD, LANES), bf16
        ),
        in_specs=[smem(), smem(), smem()] + [vmem()] * (1 + len(all_query)),
        out_specs=vmem(),
        compiler_params=params(32),
        name="attend",
    )(place, lengths, request, got_cache.reshape(n_row * page_rows, -1), *all_query)
    got = lax.all_to_all(message, "seq", 0, 0, tiled=True)

    result = pl.pallas_call(
        functools.partial(merge_kernel, scale),
        out_shape=jax.ShapeDtypeStruct((block_rows, value_dim), bf16),
        in_specs=[vmem()] * 4,
        out_specs=vmem(),
        compiler_params=params(16),
        name="merge",
    )(got, near[0], new_keys, w_uv)
    result = lax.ppermute(result, "grp", swap)
    return result.reshape(1, rows_dev, n_new, head_dev, value_dim)


def solution(mesh):
    placed = (
        P("grp", ("seq", "row"), None, None),
        P("grp", ("seq", "row"), None, None),
        P(),
        P("grp", None),
        P("grp", "row", None, "seq", None),
        P("grp", "row", None, None),
        P("seq", None, None),
        P("seq", None, None),
    )
    return jax.shard_map(
        per_device,
        mesh=mesh,
        in_specs=placed,
        out_specs=P("grp", "row", None, "seq", None),
        check_vma=False,
    )
```

```python
import functools

import jax
import jax.numpy as jnp
from jax import lax
from jax.experimental import pallas as pl
from jax.experimental.pallas import tpu as pltpu
from jax.sharding import PartitionSpec as P

FILL_LOW = -1e30
LOG2_E = 1.4426950408889634
LANES = 128
FOLD = 16
PARTS = 8
N_NEAR = 4
NT = (((1,), (1,)), ((), ()))


def smem():
    return pl.BlockSpec(memory_space=pltpu.SMEM)


def vmem():
    return pl.BlockSpec(memory_space=pltpu.VMEM)


def params(mib):
    return pltpu.CompilerParams(vmem_limit_bytes=mib << 20)


def pack_kernel(request_ref, table_ref, pool_ref, out_ref, packed, sems):
    n_peer, half_page, _ = packed.shape
    latent = packed.shape[2] // 2 - LANES // 2
    n_row = n_peer // 2
    stores = []
    for peer in range(n_peer):
        page = table_ref[0, request_ref[0, peer % n_row * 2 + peer // n_row]]
        packed[peer, :, :latent] = pool_ref[page, :half_page, :latent]
        packed[peer, :, latent : latent + LANES] = jnp.concatenate(
            [pool_ref[page, :half_page, latent:], pool_ref[page, half_page:, latent:]], axis=1
        )
        packed[peer, :, latent + LANES :] = pool_ref[page, half_page:, :latent]
        stores.append(pltpu.make_async_copy(packed.at[peer], out_ref.at[peer], sems.at[peer]))
        stores[peer].start()
    for store in stores:
        store.wait()


def query_kernel(place_ref, lengths_ref, request_ref, query_ref, w_ref, out_ref, bias_ref):
    group, seq, row = place_ref[0], place_ref[1], place_ref[2]
    heads, nope, latent = w_ref.shape
    rows = query_ref.shape[0]
    n_row = request_ref.shape[1] // 2
    keys = bias_ref.shape[1]
    half_page = keys // (2 * n_row)
    pair = seq // N_NEAR % 2
    length = lengths_ref[group, request_ref[0, row * 2 + pair]]
    key_id = lax.broadcasted_iota(jnp.int32, (1, keys), 1)
    source = key_id // half_page
    block = (seq + (source // n_row - pair) * N_NEAR) * n_row + source % n_row
    for h in range(2):
        position = block * (2 * half_page) + h * half_page + key_id % half_page
        bias_ref[h : h + 1, :] = jnp.where(position < length, 0.0, FILL_LOW)
    plain = query_ref[:, :nope]
    head_of = lax.broadcasted_iota(jnp.int32, (rows, latent), 0) % heads
    total = jnp.zeros((rows, latent), jnp.float32)
    for h in range(heads):
        one = jnp.dot(plain, w_ref[h], preferred_element_type=jnp.float32)
        total = jnp.where(head_of == h, one, total)
    total = total.astype(jnp.bfloat16)
    rope = query_ref[:, nope:]
    rope = jnp.concatenate([rope, rope], axis=1)
    for r in range(2):
        part = slice(r * rows // 2, (r + 1) * rows // 2)
        out_ref[r, :, :latent] = total[part]
        out_ref[r, :, latent:] = rope[part]


def split_bf16(value, count):
    parts = []
    for _ in range(count):
        part = value.astype(jnp.bfloat16).astype(jnp.float32)
        parts.append(part)
        value = value - part
    return parts


def attend_kernel(scale2, bias_ref, cache_ref, *refs):
    query_refs, (out_ref, score_ref, weight_ref, send_ref, sems) = refs[:-5], refs[-5:]
    seq = lax.axis_index("seq")
    n_seq = out_ref.shape[0]
    n_far = len(query_refs)
    rows = query_refs[0].shape[0] // N_NEAR
    latent = (cache_ref.shape[1] - LANES) // 2
    chunks = latent // LANES
    lane = lax.broadcasted_iota(jnp.int32, (rows, LANES), 1)
    base = PARTS * (lax.broadcasted_iota(jnp.int32, (rows, LANES), 0) // FOLD)
    far, near = seq // N_NEAR, seq % N_NEAR
    owner = [
        (far + n_far - b // N_NEAR) % n_far * N_NEAR + (near ^ (b % N_NEAR)) for b in range(n_seq)
    ]
    query = jnp.concatenate([ref[...] for ref in query_refs], axis=0)
    plain, rope = query[:, :latent], query[:, latent:]
    low = lax.broadcasted_iota(jnp.int32, rope.shape, 1) < LANES // 2
    zero = jnp.zeros_like(rope)
    for h in range(2):
        if h == 0:
            side = jnp.concatenate([plain, jnp.where(low, rope, zero)], axis=1)
        else:
            side = jnp.concatenate([jnp.where(low, zero, rope), plain], axis=1)
        score_ref[h] = lax.dot_general(
            side, cache_ref[:, h * latent : (h + 1) * latent + LANES], NT,
            preferred_element_type=jnp.float32,
        )
    for b in range(n_seq):
        block = slice(b * rows, (b + 1) * rows)
        scores = [score_ref[h, block] + bias_ref[h : h + 1, :] for h in range(2)]
        best = jnp.max(jnp.maximum(*scores), axis=1, keepdims=True)
        weights = [jnp.exp2((one - best) * scale2) for one in scores]
        for h in range(2):
            weight_ref[h, block] = weights[h].astype(jnp.bfloat16)
        weight_sum = jnp.sum(weights[0] + weights[1], axis=1, keepdims=True)
        stats = jnp.zeros((rows, LANES), jnp.float32)
        for j, part in enumerate(split_bf16(best * scale2, 3) + split_bf16(weight_sum, 2)):
            stats = jnp.where(lane == base + j, part, stats)
        stats = sum(stats[i * FOLD : (i + 1) * FOLD] for i in range(rows // FOLD))
        send_ref[b, chunks * rows :, :] = stats.astype(jnp.bfloat16)
    value = jnp.dot(weight_ref[0], cache_ref[:, :latent], preferred_element_type=jnp.float32)
    value += jnp.dot(
        weight_ref[1], cache_ref[:, latent + LANES :], preferred_element_type=jnp.float32
    )
    value = value.astype(jnp.bfloat16)
    sends = []
    for b in range(n_seq):
        for c in range(chunks):
            send_ref[b, c * rows : (c + 1) * rows, :] = (
                value[b * rows : (b + 1) * rows, c * LANES : (c + 1) * LANES]
            )
        sends.append(pltpu.make_async_copy(send_ref.at[b], out_ref.at[owner[b]], sems.at[b]))
        sends[b].start()
    for send in sends:
        send.wait()


def merge_kernel(scale2, got_ref, query_ref, new_ref, w_ref, out_ref):
    n_seq = got_ref.shape[0]
    heads, latent, _ = w_ref.shape
    rows = query_ref.shape[1]
    chunks = latent // LANES
    tail = chunks * rows
    lane = lax.broadcasted_iota(jnp.int32, (rows, LANES), 1)
    base = PARTS * (lax.broadcasted_iota(jnp.int32, (rows, LANES), 0) // FOLD)
    in_best = (lane >= base) & (lane < base + 3)
    in_sum = (lane >= base + 3) & (lane < base + 5)
    count = new_ref.shape[0] // 2
    token = lax.broadcasted_iota(jnp.int32, (rows, count), 0) // heads
    causal = lax.broadcasted_iota(jnp.int32, (rows, count), 1) <= token
    latent_out = []
    for r in range(2):
        sources = [i for i in range(n_seq) if i // N_NEAR % 2 == r]
        bests, sums = [], []
        for i in sources:
            stats = got_ref[i, tail:, :].astype(jnp.float32)
            stats = jnp.concatenate([stats] * (rows // FOLD), axis=0)
            bests.append(jnp.sum(jnp.where(in_best, stats, 0.0), axis=1, keepdims=True))
            sums.append(jnp.sum(jnp.where(in_sum, stats, 0.0), axis=1, keepdims=True))
        new_keys = new_ref[...].astype(jnp.float32)[r * count : (r + 1) * count]
        new_lat, rope = new_keys[:, :latent], new_keys[:, latent:]
        keys = jnp.concatenate([new_keys, jnp.zeros_like(rope)], axis=1).astype(jnp.bfloat16)
        new_scores = lax.dot_general(query_ref[r], keys, NT, preferred_element_type=jnp.float32)
        new_scores = jnp.where(causal, new_scores * scale2, FILL_LOW)
        best = jnp.max(new_scores, axis=1, keepdims=True)
        for one in bests:
            best = jnp.maximum(best, one)
        new_weights = jnp.where(causal, jnp.exp2(new_scores - best), 0.0)
        total = jnp.sum(new_weights, axis=1, keepdims=True)
        new_weights = new_weights.astype(jnp.bfloat16).astype(jnp.float32)
        factors = [jnp.exp2(one - best) for one in bests]
        for factor, one in zip(factors, sums):
            total = total + factor * one
        pieces = []
        for c in range(chunks):
            value = jnp.zeros((rows, LANES), jnp.float32)
            for j in range(count):
                value = value + (
                    new_weights[:, j : j + 1] * new_lat[j : j + 1, c * LANES : (c + 1) * LANES]
                )
            for factor, i in zip(factors, sources):
                value = value + factor * got_ref[i, c * rows : (c + 1) * rows].astype(jnp.float32)
            pieces.append((value / total).astype(jnp.bfloat16))
        latent_out.append(jnp.concatenate(pieces, axis=1))
    latent_out = jnp.concatenate(latent_out, axis=0)
    head_of = lax.broadcasted_iota(jnp.int32, out_ref.shape, 0) % heads
    result = jnp.zeros(out_ref.shape, jnp.float32)
    for h in range(heads):
        one = jnp.dot(latent_out, w_ref[h], preferred_element_type=jnp.float32)
        result = jnp.where(head_of == h, one, result)
    out_ref[...] = result.astype(jnp.bfloat16)


def per_device(latent_pool, block_table, lengths, row_request, queries, new_latent, w_uk, w_uv):
    n_seq = lax.axis_size("seq")
    n_row = lax.axis_size("row")
    group = lax.axis_index("grp")
    _, rows_dev, n_new, head_dev, query_width = queries.shape
    _, page_rows, lat_width = latent_pool.shape[1:]
    latent_dim = w_uk.shape[2]
    value_dim = w_uv.shape[2]
    half_rows = n_new * head_dev
    block_rows = rows_dev * half_rows
    keys = n_row * page_rows
    scale2 = query_width ** (-0.5) * LOG2_E
    swap = [(0, 1), (1, 0)]
    bf16 = jnp.bfloat16

    pool = lax.ppermute(latent_pool[0], "grp", swap)
    table = lax.ppermute(block_table.reshape(1, -1), "grp", swap)
    packed_shape = (2 * n_row, page_rows // 2, 2 * latent_dim + LANES)
    packed = pl.pallas_call(
        pack_kernel,
        out_shape=jax.ShapeDtypeStruct(packed_shape, bf16),
        in_specs=[smem(), smem(), vmem()],
        out_specs=pl.BlockSpec(memory_space=pl.ANY),
        scratch_shapes=[pltpu.VMEM(packed_shape, bf16), pltpu.SemaphoreType.DMA((2 * n_row,))],
        compiler_params=params(16),
        name="pack",
    )(row_request, table, pool)
    pairs = [
        [(base + pair * N_NEAR) * n_row + row for pair in range(2) for row in range(n_row)]
        for base in range(n_seq)
        if base // N_NEAR % 2 == 0
    ]
    got_cache = lax.all_to_all(
        packed, ("seq", "row"), 0, 0, axis_index_groups=pairs, tiled=True
    )

    place = jnp.stack([1 - group, lax.axis_index("seq"), lax.axis_index("row")]).astype(jnp.int32)
    own_query, bias = pl.pallas_call(
        query_kernel,
        out_shape=(
            jax.ShapeDtypeStruct((rows_dev, half_rows, latent_dim + LANES), bf16),
            jax.ShapeDtypeStruct((2, keys), jnp.float32),
        ),
        in_specs=[smem()] * 3 + [vmem()] * 2,
        out_specs=(vmem(), vmem()),
        compiler_params=params(16),
        name="query",
    )(place, lengths, row_request, queries.reshape(block_rows, query_width), w_uk)
    near = [own_query]
    for k in range(1, N_NEAR):
        near.append(lax.ppermute(own_query, "seq", [(s, s ^ k) for s in range(n_seq)]))
    near_query = jnp.concatenate(near, axis=1)
    pair = lax.axis_index("seq") // N_NEAR % 2
    same, other = (
        lax.dynamic_index_in_dim(near_query, one, 0, keepdims=False) for one in (pair, 1 - pair)
    )
    all_query = [same]
    for j in range(1, n_seq // N_NEAR):
        route = [(s, (s + j * N_NEAR) % n_seq) for s in range(n_seq)]
        all_query.append(lax.ppermute(other if j % 2 else same, "seq", route))

    send_shape = (n_seq, half_rows * latent_dim // LANES + FOLD, LANES)
    message = pl.pallas_call(
        functools.partial(attend_kernel, scale2),
        out_shape=jax.ShapeDtypeStruct(send_shape, bf16),
        in_specs=[vmem()] * (2 + len(all_query)),
        out_specs=pl.BlockSpec(memory_space=pl.ANY),
        scratch_shapes=[
            pltpu.VMEM((2, n_seq * half_rows, keys), jnp.float32),
            pltpu.VMEM((2, n_seq * half_rows, keys), bf16),
            pltpu.VMEM(send_shape, bf16),
            pltpu.SemaphoreType.DMA((n_seq,)),
        ],
        compiler_params=params(32),
        name="attend",
    )(bias, got_cache.reshape(keys, -1), *all_query)
    got = lax.all_to_all(message, "seq", 0, 0, tiled=True)

    result = pl.pallas_call(
        functools.partial(merge_kernel, scale2),
        out_shape=jax.ShapeDtypeStruct((block_rows, value_dim), bf16),
        in_specs=[vmem()] * 4,
        out_specs=vmem(),
        compiler_params=params(16),
        name="merge",
    )(got, own_query, new_latent.reshape(rows_dev * n_new, lat_width), w_uv)
    return result.reshape(1, rows_dev, n_new, head_dev, value_dim)


def solution(mesh):
    placed = (
        P("grp", ("seq", "row"), None, None),
        P("grp", ("seq", "row"), None, None),
        P(),
        P("grp", None),
        P("grp", "row", None, "seq", None),
        P("grp", "row", None, None),
        P("seq", None, None),
        P("seq", None, None),
    )
    return jax.shard_map(
        per_device,
        mesh=mesh,
        in_specs=placed,
        out_specs=P("grp", "row", None, "seq", None),
        check_vma=False,
    )
```

```python
import functools

import jax
import jax.numpy as jnp
from jax import lax
from jax.experimental import pallas as pl
from jax.experimental.pallas import tpu as pltpu
from jax.sharding import PartitionSpec as P

FILL_LOW = -1e30
LOG2_E = 1.4426950408889634
LANES = 128
FOLD = 16
PARTS = 8
N_NEAR = 4
NT = (((1,), (1,)), ((), ()))


def smem():
    return pl.BlockSpec(memory_space=pltpu.SMEM)


def vmem():
    return pl.BlockSpec(memory_space=pltpu.VMEM)


def params(mib):
    return pltpu.CompilerParams(vmem_limit_bytes=mib << 20)


def pack_kernel(request_ref, table_ref, pool_ref, out_ref, packed, sems):
    n_peer, half_page, _ = packed.shape
    latent = packed.shape[2] // 2 - LANES // 2
    n_row = n_peer // 2
    stores = []
    for peer in range(n_peer):
        page = table_ref[0, request_ref[0, peer % n_row * 2 + peer // n_row]]
        packed[peer, :, :latent] = pool_ref[page, :half_page, :latent]
        packed[peer, :, latent : latent + LANES] = jnp.concatenate(
            [pool_ref[page, :half_page, latent:], pool_ref[page, half_page:, latent:]], axis=1
        )
        packed[peer, :, latent + LANES :] = pool_ref[page, half_page:, :latent]
        stores.append(pltpu.make_async_copy(packed.at[peer], out_ref.at[peer], sems.at[peer]))
        stores[peer].start()
    for store in stores:
        store.wait()


def query_kernel(place_ref, lengths_ref, request_ref, query_ref, w_ref, out_ref, bias_ref):
    group, seq, row = place_ref[0], place_ref[1], place_ref[2]
    heads, nope, latent = w_ref.shape
    rows = query_ref.shape[0]
    n_row = request_ref.shape[1] // 2
    keys = bias_ref.shape[1]
    half_page = keys // (2 * n_row)
    pair = seq // N_NEAR % 2
    length = lengths_ref[group, request_ref[0, row * 2 + pair]]
    key_id = lax.broadcasted_iota(jnp.int32, (1, keys), 1)
    source = key_id // half_page
    block = (seq + (source // n_row - pair) * N_NEAR) * n_row + source % n_row
    for h in range(2):
        position = block * (2 * half_page) + h * half_page + key_id % half_page
        bias_ref[h : h + 1, :] = jnp.where(position < length, 0.0, FILL_LOW)
    plain = query_ref[:, :nope]
    head_of = lax.broadcasted_iota(jnp.int32, (rows, latent), 0) % heads
    total = jnp.zeros((rows, latent), jnp.float32)
    for h in range(heads):
        one = jnp.dot(plain, w_ref[h], preferred_element_type=jnp.float32)
        total = jnp.where(head_of == h, one, total)
    total = total.astype(jnp.bfloat16)
    rope = query_ref[:, nope:]
    rope = jnp.concatenate([rope, rope], axis=1)
    for r in range(2):
        part = slice(r * rows // 2, (r + 1) * rows // 2)
        out_ref[r, :, :latent] = total[part]
        out_ref[r, :, latent:] = rope[part]


def split_bf16(value, count):
    parts = []
    for _ in range(count):
        part = value.astype(jnp.bfloat16).astype(jnp.float32)
        parts.append(part)
        value = value - part
    return parts


def attend_kernel(scale2, bias_ref, cache_ref, *refs):
    query_refs, (out_ref, score_ref, weight_ref, send_ref, sems) = refs[:-5], refs[-5:]
    seq = lax.axis_index("seq")
    n_seq = out_ref.shape[0]
    n_far = len(query_refs)
    rows = query_refs[0].shape[0] // N_NEAR
    latent = (cache_ref.shape[1] - LANES) // 2
    chunks = latent // LANES
    lane = lax.broadcasted_iota(jnp.int32, (rows, LANES), 1)
    base = PARTS * (lax.broadcasted_iota(jnp.int32, (rows, LANES), 0) // FOLD)
    far, near = seq // N_NEAR, seq % N_NEAR
    owner = [
        (far + n_far - b // N_NEAR) % n_far * N_NEAR + (near ^ (b % N_NEAR)) for b in range(n_seq)
    ]
    query = jnp.concatenate([ref[...] for ref in query_refs], axis=0)
    plain, rope = query[:, :latent], query[:, latent:]
    low = lax.broadcasted_iota(jnp.int32, rope.shape, 1) < LANES // 2
    zero = jnp.zeros_like(rope)
    for h in range(2):
        if h == 0:
            side = jnp.concatenate([plain, jnp.where(low, rope, zero)], axis=1)
        else:
            side = jnp.concatenate([jnp.where(low, zero, rope), plain], axis=1)
        score_ref[h] = lax.dot_general(
            side, cache_ref[:, h * latent : (h + 1) * latent + LANES], NT,
            preferred_element_type=jnp.float32,
        )
    for b in range(n_seq):
        block = slice(b * rows, (b + 1) * rows)
        scores = [score_ref[h, block] + bias_ref[h : h + 1, :] for h in range(2)]
        best = jnp.max(jnp.maximum(*scores), axis=1, keepdims=True)
        weights = [jnp.exp2((one - best) * scale2) for one in scores]
        for h in range(2):
            weight_ref[h, block] = weights[h].astype(jnp.bfloat16)
        weight_sum = jnp.sum(weights[0] + weights[1], axis=1, keepdims=True)
        stats = jnp.zeros((rows, LANES), jnp.float32)
        for j, part in enumerate(split_bf16(best * scale2, 3) + split_bf16(weight_sum, 2)):
            stats = jnp.where(lane == base + j, part, stats)
        stats = sum(stats[i * FOLD : (i + 1) * FOLD] for i in range(rows // FOLD))
        send_ref[b, chunks * rows :, :] = stats.astype(jnp.bfloat16)
    value = jnp.dot(weight_ref[0], cache_ref[:, :latent], preferred_element_type=jnp.float32)
    value += jnp.dot(
        weight_ref[1], cache_ref[:, latent + LANES :], preferred_element_type=jnp.float32
    )
    value = value.astype(jnp.bfloat16)
    sends = []
    for b in range(n_seq):
        for c in range(chunks):
            send_ref[b, c * rows : (c + 1) * rows, :] = (
                value[b * rows : (b + 1) * rows, c * LANES : (c + 1) * LANES]
            )
        sends.append(pltpu.make_async_copy(send_ref.at[b], out_ref.at[owner[b]], sems.at[b]))
        sends[b].start()
    for send in sends:
        send.wait()


def fresh_kernel(scale2, query_ref, new_ref, best_ref, sum_ref, value_ref):
    rows, width = query_ref.shape[1:]
    latent = width - LANES
    count = new_ref.shape[0] // 2
    heads = rows // count
    token = lax.broadcasted_iota(jnp.int32, (rows, count), 0) // heads
    causal = lax.broadcasted_iota(jnp.int32, (rows, count), 1) <= token
    for r in range(2):
        part = slice(r * rows, (r + 1) * rows)
        mine = new_ref[...].astype(jnp.float32)[r * count : (r + 1) * count]
        new_lat, rope = mine[:, :latent], mine[:, latent:]
        keys = jnp.concatenate([mine, jnp.zeros_like(rope)], axis=1).astype(jnp.bfloat16)
        scores = lax.dot_general(query_ref[r], keys, NT, preferred_element_type=jnp.float32)
        scores = jnp.where(causal, scores * scale2, FILL_LOW)
        best = jnp.max(scores, axis=1, keepdims=True)
        weights = jnp.exp2(scores - best)
        best_ref[part] = jnp.broadcast_to(best, (rows, LANES))
        sum_ref[part] = jnp.broadcast_to(jnp.sum(weights, axis=1, keepdims=True), (rows, LANES))
        weights = weights.astype(jnp.bfloat16).astype(jnp.float32)
        value = weights[:, :1] * new_lat[:1]
        for j in range(1, count):
            value = value + weights[:, j : j + 1] * new_lat[j : j + 1]
        value_ref[part] = value


def merge_kernel(got_ref, best_ref, sum_ref, value_ref, w_ref, out_ref):
    n_seq = got_ref.shape[0]
    heads, latent, _ = w_ref.shape
    rows = best_ref.shape[0] // 2
    chunks = latent // LANES
    tail = chunks * rows
    lane = lax.broadcasted_iota(jnp.int32, (rows, LANES), 1)
    base = PARTS * (lax.broadcasted_iota(jnp.int32, (rows, LANES), 0) // FOLD)
    in_best = (lane >= base) & (lane < base + 3)
    in_sum = (lane >= base + 3) & (lane < base + 5)
    latent_out = []
    for r in range(2):
        part = slice(r * rows, (r + 1) * rows)
        sources = [i for i in range(n_seq) if i // N_NEAR % 2 == r]
        bests, sums = [], []
        for i in sources:
            stats = got_ref[i, tail:, :].astype(jnp.float32)
            stats = jnp.concatenate([stats] * (rows // FOLD), axis=0)
            bests.append(jnp.sum(jnp.where(in_best, stats, 0.0), axis=1, keepdims=True))
            sums.append(jnp.sum(jnp.where(in_sum, stats, 0.0), axis=1, keepdims=True))
        fresh_best = best_ref[part]
        best = fresh_best
        for one in bests:
            best = jnp.maximum(best, one)
        fresh_factor = jnp.exp2(fresh_best - best)
        factors = [jnp.exp2(one - best) for one in bests]
        total = fresh_factor * sum_ref[part]
        for factor, one in zip(factors, sums):
            total = total + factor * one
        inverse = 1.0 / total
        pieces = []
        for c in range(chunks):
            value = fresh_factor * value_ref[part, c * LANES : (c + 1) * LANES]
            for factor, i in zip(factors, sources):
                value = value + factor * got_ref[i, c * rows : (c + 1) * rows].astype(jnp.float32)
            pieces.append((value * inverse).astype(jnp.bfloat16))
        latent_out.append(jnp.concatenate(pieces, axis=1))
    latent_out = jnp.concatenate(latent_out, axis=0)
    head_of = lax.broadcasted_iota(jnp.int32, out_ref.shape, 0) % heads
    result = jnp.zeros(out_ref.shape, jnp.float32)
    for h in range(heads):
        one = jnp.dot(latent_out, w_ref[h], preferred_element_type=jnp.float32)
        result = jnp.where(head_of == h, one, result)
    out_ref[...] = result.astype(jnp.bfloat16)


def per_device(latent_pool, block_table, lengths, row_request, queries, new_latent, w_uk, w_uv):
    n_seq = lax.axis_size("seq")
    n_row = lax.axis_size("row")
    group = lax.axis_index("grp")
    _, rows_dev, n_new, head_dev, query_width = queries.shape
    _, page_rows, lat_width = latent_pool.shape[1:]
    latent_dim = w_uk.shape[2]
    value_dim = w_uv.shape[2]
    half_rows = n_new * head_dev
    block_rows = rows_dev * half_rows
    keys = n_row * page_rows
    scale2 = query_width ** (-0.5) * LOG2_E
    swap = [(0, 1), (1, 0)]
    bf16 = jnp.bfloat16

    pool = lax.ppermute(latent_pool[0], "grp", swap)
    table = lax.ppermute(block_table.reshape(1, -1), "grp", swap)
    order = jnp.clip(row_request, 0, row_request.shape[1] - 1)
    packed_shape = (2 * n_row, page_rows // 2, 2 * latent_dim + LANES)
    packed = pl.pallas_call(
        pack_kernel,
        out_shape=jax.ShapeDtypeStruct(packed_shape, bf16),
        in_specs=[smem(), smem(), vmem()],
        out_specs=pl.BlockSpec(memory_space=pl.ANY),
        scratch_shapes=[pltpu.VMEM(packed_shape, bf16), pltpu.SemaphoreType.DMA((2 * n_row,))],
        compiler_params=params(16),
        name="pack",
    )(order, table, pool)
    pairs = [
        [(base + pair * N_NEAR) * n_row + row for pair in range(2) for row in range(n_row)]
        for base in range(n_seq)
        if base // N_NEAR % 2 == 0
    ]
    got_cache = lax.all_to_all(
        packed, ("seq", "row"), 0, 0, axis_index_groups=pairs, tiled=True
    )

    place = jnp.stack([1 - group, lax.axis_index("seq"), lax.axis_index("row")]).astype(jnp.int32)
    own_query, bias = pl.pallas_call(
        query_kernel,
        out_shape=(
            jax.ShapeDtypeStruct((rows_dev, half_rows, latent_dim + LANES), bf16),
            jax.ShapeDtypeStruct((2, keys), jnp.float32),
        ),
        in_specs=[smem()] * 3 + [vmem()] * 2,
        out_specs=(vmem(), vmem()),
        compiler_params=params(16),
        name="query",
    )(place, lengths, row_request, queries.reshape(block_rows, query_width), w_uk)
    near = [own_query]
    for k in range(1, N_NEAR):
        near.append(lax.ppermute(own_query, "seq", [(s, s ^ k) for s in range(n_seq)]))
    near_query = jnp.concatenate(near, axis=1)
    pair = lax.axis_index("seq") // N_NEAR % 2
    same, other = (
        lax.dynamic_index_in_dim(near_query, one, 0, keepdims=False) for one in (pair, 1 - pair)
    )
    all_query = [same]
    for j in range(1, n_seq // N_NEAR):
        route = [(s, (s + j * N_NEAR) % n_seq) for s in range(n_seq)]
        all_query.append(lax.ppermute(other if j % 2 else same, "seq", route))

    send_shape = (n_seq, half_rows * latent_dim // LANES + FOLD, LANES)
    message = pl.pallas_call(
        functools.partial(attend_kernel, scale2),
        out_shape=jax.ShapeDtypeStruct(send_shape, bf16),
        in_specs=[vmem()] * (2 + len(all_query)),
        out_specs=pl.BlockSpec(memory_space=pl.ANY),
        scratch_shapes=[
            pltpu.VMEM((2, n_seq * half_rows, keys), jnp.float32),
            pltpu.VMEM((2, n_seq * half_rows, keys), bf16),
            pltpu.VMEM(send_shape, bf16),
            pltpu.SemaphoreType.DMA((n_seq,)),
        ],
        compiler_params=params(32),
        name="attend",
    )(bias, got_cache.reshape(keys, -1), *all_query)
    got = lax.all_to_all(message, "seq", 0, 0, tiled=True)

    fresh = pl.pallas_call(
        functools.partial(fresh_kernel, scale2),
        out_shape=[
            jax.ShapeDtypeStruct((block_rows, width), jnp.float32)
            for width in (LANES, LANES, latent_dim)
        ],
        in_specs=[vmem()] * 2,
        out_specs=[vmem()] * 3,
        compiler_params=params(16),
        name="fresh",
    )(own_query, new_latent.reshape(rows_dev * n_new, lat_width))
    result = pl.pallas_call(
        merge_kernel,
        out_shape=jax.ShapeDtypeStruct((block_rows, value_dim), bf16),
        in_specs=[vmem()] * 5,
        out_specs=vmem(),
        compiler_params=params(16),
        name="merge",
    )(got, *fresh, w_uv)
    return result.reshape(1, rows_dev, n_new, head_dev, value_dim)


def solution(mesh):
    placed = (
        P("grp", ("seq", "row"), None, None),
        P("grp", ("seq", "row"), None, None),
        P(),
        P("grp", None),
        P("grp", "row", None, "seq", None),
        P("grp", "row", None, None),
        P("seq", None, None),
        P("seq", None, None),
    )
    return jax.shard_map(
        per_device,
        mesh=mesh,
        in_specs=placed,
        out_specs=P("grp", "row", None, "seq", None),
        check_vma=False,
    )
```

```python
import functools

import jax
import jax.numpy as jnp
from jax import lax
from jax.experimental import pallas as pl
from jax.experimental.pallas import tpu as pltpu
from jax.sharding import PartitionSpec as P

FILL_LOW = -1e30
LOG2_E = 1.4426950408889634
LANES = 128
FOLD = 16
PARTS = 8
N_NEAR = 4
NT = (((1,), (1,)), ((), ()))


def smem():
    return pl.BlockSpec(memory_space=pltpu.SMEM)


def vmem():
    return pl.BlockSpec(memory_space=pltpu.VMEM)


def params(mib):
    return pltpu.CompilerParams(vmem_limit_bytes=mib << 20)


def pack_kernel(request_ref, table_ref, pool_ref, out_ref, packed, sems):
    n_peer, half_page, _ = packed.shape
    latent = packed.shape[2] // 2 - LANES // 2
    n_row = n_peer // 2
    stores = []
    for peer in range(n_peer):
        page = table_ref[0, request_ref[0, peer % n_row * 2 + peer // n_row]]
        packed[peer, :, :latent] = pool_ref[page, :half_page, :latent]
        packed[peer, :, latent : latent + LANES] = jnp.concatenate(
            [pool_ref[page, :half_page, latent:], pool_ref[page, half_page:, latent:]], axis=1
        )
        packed[peer, :, latent + LANES :] = pool_ref[page, half_page:, :latent]
        stores.append(pltpu.make_async_copy(packed.at[peer], out_ref.at[peer], sems.at[peer]))
        stores[peer].start()
    for store in stores:
        store.wait()


def query_kernel(place_ref, lengths_ref, request_ref, query_ref, w_ref, out_ref, bias_ref):
    group, seq, row = place_ref[0], place_ref[1], place_ref[2]
    heads, nope, latent = w_ref.shape
    rows = query_ref.shape[0]
    n_row = request_ref.shape[1] // 2
    keys = bias_ref.shape[1]
    half_page = keys // (2 * n_row)
    pair = seq % 2
    length = lengths_ref[group, request_ref[0, row * 2 + pair]]
    key_id = lax.broadcasted_iota(jnp.int32, (1, keys), 1)
    source = key_id // half_page
    block = (seq - pair + source // n_row) * n_row + source % n_row
    for h in range(2):
        position = block * (2 * half_page) + h * half_page + key_id % half_page
        bias_ref[h : h + 1, :] = jnp.where(position < length, 0.0, FILL_LOW)
    plain = query_ref[:, :nope]
    head_of = lax.broadcasted_iota(jnp.int32, (rows, latent), 0) % heads
    total = jnp.zeros((rows, latent), jnp.float32)
    for h in range(heads):
        one = jnp.dot(plain, w_ref[h], preferred_element_type=jnp.float32)
        total = jnp.where(head_of == h, one, total)
    total = total.astype(jnp.bfloat16)
    rope = query_ref[:, nope:]
    rope = jnp.concatenate([rope, rope], axis=1)
    for r in range(2):
        part = slice(r * rows // 2, (r + 1) * rows // 2)
        out_ref[r, :, :latent] = total[part]
        out_ref[r, :, latent:] = rope[part]


def split_bf16(value, count):
    parts = []
    for _ in range(count):
        part = value.astype(jnp.bfloat16).astype(jnp.float32)
        parts.append(part)
        value = value - part
    return parts


def attend_kernel(scale2, bias_ref, cache_ref, *refs):
    query_refs, (out_ref, score_ref, weight_ref) = refs[:-3], refs[-3:]
    seq = lax.axis_index("seq")
    n_seq = out_ref.shape[0]
    n_far = len(query_refs)
    rows = query_refs[0].shape[0] // N_NEAR
    latent = (cache_ref.shape[1] - LANES) // 2
    chunks = latent // LANES
    lane = lax.broadcasted_iota(jnp.int32, (rows, LANES), 1)
    base = PARTS * (lax.broadcasted_iota(jnp.int32, (rows, LANES), 0) // FOLD)
    far, near = seq // N_NEAR, seq % N_NEAR
    owner = [
        (far + n_far - b // N_NEAR) % n_far * N_NEAR + (near ^ (b % N_NEAR)) for b in range(n_seq)
    ]
    query = jnp.concatenate([ref[...] for ref in query_refs], axis=0)
    plain, rope = query[:, :latent], query[:, latent:]
    low = lax.broadcasted_iota(jnp.int32, rope.shape, 1) < LANES // 2
    zero = jnp.zeros_like(rope)
    for h in range(2):
        if h == 0:
            side = jnp.concatenate([plain, jnp.where(low, rope, zero)], axis=1)
        else:
            side = jnp.concatenate([jnp.where(low, zero, rope), plain], axis=1)
        score_ref[h] = lax.dot_general(
            side, cache_ref[:, h * latent : (h + 1) * latent + LANES], NT,
            preferred_element_type=jnp.float32,
        )
    for b in range(n_seq):
        block = slice(b * rows, (b + 1) * rows)
        scores = [score_ref[h, block] + bias_ref[h : h + 1, :] for h in range(2)]
        best = jnp.max(jnp.maximum(*scores), axis=1, keepdims=True)
        weights = [jnp.exp2((one - best) * scale2) for one in scores]
        for h in range(2):
            weight_ref[h, block] = weights[h].astype(jnp.bfloat16)
        weight_sum = jnp.sum(weights[0] + weights[1], axis=1, keepdims=True)
        stats = jnp.zeros((rows, LANES), jnp.float32)
        for j, part in enumerate(split_bf16(best * scale2, 3) + split_bf16(weight_sum, 2)):
            stats = jnp.where(lane == base + j, part, stats)
        stats = sum(stats[i * FOLD : (i + 1) * FOLD] for i in range(rows // FOLD))
        out_ref[owner[b], chunks * rows :, :] = stats.astype(jnp.bfloat16)
    value = jnp.dot(weight_ref[0], cache_ref[:, :latent], preferred_element_type=jnp.float32)
    value += jnp.dot(
        weight_ref[1], cache_ref[:, latent + LANES :], preferred_element_type=jnp.float32
    )
    value = value.astype(jnp.bfloat16)
    for b in range(n_seq):
        for c in range(chunks):
            out_ref[owner[b], c * rows : (c + 1) * rows, :] = (
                value[b * rows : (b + 1) * rows, c * LANES : (c + 1) * LANES]
            )


def fresh_kernel(scale2, query_ref, new_ref, best_ref, sum_ref, value_ref):
    rows, width = query_ref.shape[1:]
    latent = width - LANES
    count = new_ref.shape[0] // 2
    heads = rows // count
    token = lax.broadcasted_iota(jnp.int32, (rows, count), 0) // heads
    causal = lax.broadcasted_iota(jnp.int32, (rows, count), 1) <= token
    for r in range(2):
        part = slice(r * rows, (r + 1) * rows)
        mine = new_ref[...].astype(jnp.float32)[r * count : (r + 1) * count]
        new_lat, rope = mine[:, :latent], mine[:, latent:]
        keys = jnp.concatenate([mine, jnp.zeros_like(rope)], axis=1).astype(jnp.bfloat16)
        scores = lax.dot_general(query_ref[r], keys, NT, preferred_element_type=jnp.float32)
        scores = jnp.where(causal, scores * scale2, FILL_LOW)
        best = jnp.max(scores, axis=1, keepdims=True)
        weights = jnp.exp2(scores - best)
        best_ref[part] = jnp.broadcast_to(best, (rows, LANES))
        sum_ref[part] = jnp.broadcast_to(jnp.sum(weights, axis=1, keepdims=True), (rows, LANES))
        weights = weights.astype(jnp.bfloat16).astype(jnp.float32)
        value = weights[:, :1] * new_lat[:1]
        for j in range(1, count):
            value = value + weights[:, j : j + 1] * new_lat[j : j + 1]
        value_ref[part] = value


def merge_kernel(got_ref, best_ref, sum_ref, value_ref, w_ref, out_ref):
    n_seq = got_ref.shape[0]
    heads, latent, _ = w_ref.shape
    rows = best_ref.shape[0] // 2
    chunks = latent // LANES
    tail = chunks * rows
    lane = lax.broadcasted_iota(jnp.int32, (rows, LANES), 1)
    base = PARTS * (lax.broadcasted_iota(jnp.int32, (rows, LANES), 0) // FOLD)
    in_best = (lane >= base) & (lane < base + 3)
    in_sum = (lane >= base + 3) & (lane < base + 5)
    latent_out = []
    for r in range(2):
        part = slice(r * rows, (r + 1) * rows)
        sources = range(r, n_seq, 2)
        bests, sums = [], []
        for i in sources:
            stats = got_ref[i, tail:, :].astype(jnp.float32)
            stats = jnp.concatenate([stats] * (rows // FOLD), axis=0)
            bests.append(jnp.sum(jnp.where(in_best, stats, 0.0), axis=1, keepdims=True))
            sums.append(jnp.sum(jnp.where(in_sum, stats, 0.0), axis=1, keepdims=True))
        fresh_best = best_ref[part]
        best = fresh_best
        for one in bests:
            best = jnp.maximum(best, one)
        fresh_factor = jnp.exp2(fresh_best - best)
        factors = [jnp.exp2(one - best) for one in bests]
        total = fresh_factor * sum_ref[part]
        for factor, one in zip(factors, sums):
            total = total + factor * one
        inverse = 1.0 / total
        pieces = []
        for c in range(chunks):
            value = fresh_factor * value_ref[part, c * LANES : (c + 1) * LANES]
            for factor, i in zip(factors, sources):
                value = value + factor * got_ref[i, c * rows : (c + 1) * rows].astype(jnp.float32)
            pieces.append((value * inverse).astype(jnp.bfloat16))
        latent_out.append(jnp.concatenate(pieces, axis=1))
    latent_out = jnp.concatenate(latent_out, axis=0)
    head_of = lax.broadcasted_iota(jnp.int32, out_ref.shape, 0) % heads
    result = jnp.zeros(out_ref.shape, jnp.float32)
    for h in range(heads):
        one = jnp.dot(latent_out, w_ref[h], preferred_element_type=jnp.float32)
        result = jnp.where(head_of == h, one, result)
    out_ref[...] = result.astype(jnp.bfloat16)


def per_device(latent_pool, block_table, lengths, row_request, queries, new_latent, w_uk, w_uv):
    n_seq = lax.axis_size("seq")
    n_row = lax.axis_size("row")
    group = lax.axis_index("grp")
    _, rows_dev, n_new, head_dev, query_width = queries.shape
    _, page_rows, lat_width = latent_pool.shape[1:]
    latent_dim = w_uk.shape[2]
    value_dim = w_uv.shape[2]
    half_rows = n_new * head_dev
    block_rows = rows_dev * half_rows
    keys = n_row * page_rows
    scale2 = query_width ** (-0.5) * LOG2_E
    swap = [(0, 1), (1, 0)]
    bf16 = jnp.bfloat16

    pool = lax.ppermute(latent_pool[0], "grp", swap)
    table = lax.ppermute(block_table.reshape(1, -1), "grp", swap)
    order = jnp.clip(row_request, 0, row_request.shape[1] - 1)
    packed_shape = (2 * n_row, page_rows // 2, 2 * latent_dim + LANES)
    packed = pl.pallas_call(
        pack_kernel,
        out_shape=jax.ShapeDtypeStruct(packed_shape, bf16),
        in_specs=[smem(), smem(), vmem()],
        out_specs=pl.BlockSpec(memory_space=pl.ANY),
        scratch_shapes=[pltpu.VMEM(packed_shape, bf16), pltpu.SemaphoreType.DMA((2 * n_row,))],
        compiler_params=params(16),
        name="pack",
    )(order, table, pool)
    pairs = [
        [(base + pair) * n_row + row for pair in range(2) for row in range(n_row)]
        for base in range(0, n_seq, 2)
    ]
    got_cache = lax.all_to_all(
        packed, ("seq", "row"), 0, 0, axis_index_groups=pairs, tiled=True
    )

    place = jnp.stack([1 - group, lax.axis_index("seq"), lax.axis_index("row")]).astype(jnp.int32)
    own_query, bias = pl.pallas_call(
        query_kernel,
        out_shape=(
            jax.ShapeDtypeStruct((rows_dev, half_rows, latent_dim + LANES), bf16),
            jax.ShapeDtypeStruct((2, keys), jnp.float32),
        ),
        in_specs=[smem()] * 3 + [vmem()] * 2,
        out_specs=(vmem(), vmem()),
        compiler_params=params(16),
        name="query",
    )(place, lengths, row_request, queries.reshape(block_rows, query_width), w_uk)
    pair = lax.axis_index("seq") % 2
    same, other = (
        lax.dynamic_index_in_dim(own_query, one, 0, keepdims=False) for one in (pair, 1 - pair)
    )
    near = [same]
    for k in range(1, N_NEAR):
        route = [(s, s ^ k) for s in range(n_seq)]
        near.append(lax.ppermute(other if k % 2 else same, "seq", route))
    near_query = jnp.concatenate(near, axis=0)
    all_query = [near_query]
    for j in range(1, n_seq // N_NEAR):
        route = [(s, (s + j * N_NEAR) % n_seq) for s in range(n_seq)]
        all_query.append(lax.ppermute(near_query, "seq", route))

    fresh = pl.pallas_call(
        functools.partial(fresh_kernel, scale2),
        out_shape=[
            jax.ShapeDtypeStruct((block_rows, width), jnp.float32)
            for width in (LANES, LANES, latent_dim)
        ],
        in_specs=[vmem()] * 2,
        out_specs=[vmem()] * 3,
        compiler_params=params(16),
        name="fresh",
    )(own_query, new_latent.reshape(rows_dev * n_new, lat_width))
    all_query, fresh = lax.optimization_barrier((all_query, fresh))

    send_shape = (n_seq, half_rows * latent_dim // LANES + FOLD, LANES)
    message = pl.pallas_call(
        functools.partial(attend_kernel, scale2),
        out_shape=jax.ShapeDtypeStruct(send_shape, bf16),
        in_specs=[vmem()] * (2 + len(all_query)),
        out_specs=vmem(),
        scratch_shapes=[
            pltpu.VMEM((2, n_seq * half_rows, keys), jnp.float32),
            pltpu.VMEM((2, n_seq * half_rows, keys), bf16),
        ],
        compiler_params=params(32),
        name="attend",
    )(bias, got_cache.reshape(keys, -1), *all_query)
    got = lax.all_to_all(message, "seq", 0, 0, tiled=True)

    result = pl.pallas_call(
        merge_kernel,
        out_shape=jax.ShapeDtypeStruct((block_rows, value_dim), bf16),
        in_specs=[vmem()] * 5,
        out_specs=vmem(),
        compiler_params=params(16),
        name="merge",
    )(got, *fresh, w_uv)
    return result.reshape(1, rows_dev, n_new, head_dev, value_dim)


def solution(mesh):
    placed = (
        P("grp", ("seq", "row"), None, None),
        P("grp", ("seq", "row"), None, None),
        P(),
        P("grp", None),
        P("grp", "row", None, "seq", None),
        P("grp", "row", None, None),
        P("seq", None, None),
        P("seq", None, None),
    )
    return jax.shard_map(
        per_device,
        mesh=mesh,
        in_specs=placed,
        out_specs=P("grp", "row", None, "seq", None),
        check_vma=False,
    )
```

```python
import functools

import jax
import jax.numpy as jnp
from jax import lax
from jax.experimental import pallas as pl
from jax.experimental.pallas import tpu as pltpu
from jax.sharding import PartitionSpec as P

FILL_LOW = -(2.0**100)
LOG2_E = 1.4426950408889634
LANES = 128
FOLD = 16
PARTS = 8
N_NEAR = 4
NT = (((1,), (1,)), ((), ()))


def smem():
    return pl.BlockSpec(memory_space=pltpu.SMEM)


def vmem():
    return pl.BlockSpec(memory_space=pltpu.VMEM)


def params(mib):
    return pltpu.CompilerParams(vmem_limit_bytes=mib << 20)


def pack_kernel(request_ref, table_ref, pool_ref, packed):
    n_peer, half_page, _ = packed.shape
    latent = packed.shape[2] // 2 - LANES // 2
    n_row = n_peer // 2
    for peer in range(n_peer):
        page = table_ref[0, request_ref[0, peer % n_row * 2 + peer // n_row]]
        packed[peer, :, :latent] = pool_ref[page, :half_page, :latent]
        packed[peer, :, latent : latent + LANES] = jnp.concatenate(
            [pool_ref[page, :half_page, latent:], pool_ref[page, half_page:, latent:]], axis=1
        )
        packed[peer, :, latent + LANES :] = pool_ref[page, half_page:, :latent]


def query_kernel(place_ref, lengths_ref, request_ref, query_ref, w_ref, out_ref, bias_ref):
    group, seq, row = place_ref[0], place_ref[1], place_ref[2]
    heads, nope, latent = w_ref.shape
    rows = query_ref.shape[0]
    n_row = request_ref.shape[1] // 2
    keys = bias_ref.shape[1]
    half_page = keys // (2 * n_row)
    pair = seq // N_NEAR % 2
    length = lengths_ref[group, request_ref[0, row * 2 + pair]]
    key_id = lax.broadcasted_iota(jnp.int32, (1, keys), 1)
    source = key_id // half_page
    block = (seq + (source // n_row - pair) * N_NEAR) * n_row + source % n_row
    for h in range(2):
        position = block * (2 * half_page) + h * half_page + key_id % half_page
        bias_ref[h : h + 1, :] = jnp.where(position < length, 0.0, FILL_LOW)
    plain = query_ref[:, :nope]
    head_of = lax.broadcasted_iota(jnp.int32, (rows, latent), 0) % heads
    total = jnp.zeros((rows, latent), jnp.float32)
    for h in range(heads):
        one = jnp.dot(plain, w_ref[h], preferred_element_type=jnp.float32)
        total = jnp.where(head_of == h, one, total)
    total = total.astype(jnp.bfloat16)
    rope = query_ref[:, nope:]
    rope = jnp.concatenate([rope, rope], axis=1)
    for r in range(2):
        part = slice(r * rows // 2, (r + 1) * rows // 2)
        out_ref[r, :, :latent] = total[part]
        out_ref[r, :, latent:] = rope[part]


def split_bf16(value, count):
    parts = []
    for _ in range(count):
        part = value.astype(jnp.bfloat16).astype(jnp.float32)
        parts.append(part)
        value = value - part
    return parts


def side_kernel(*refs):
    query_refs, side_ref = refs[:-1], refs[-1]
    seq = lax.axis_index("seq")
    n_far = len(query_refs)
    rows = query_refs[0].shape[0] // N_NEAR
    latent = side_ref.shape[2] - LANES
    low = lax.broadcasted_iota(jnp.int32, (rows, LANES), 1) < LANES // 2
    near, far = seq // N_NEAR, seq % N_NEAR
    for j in range(n_far):
        for k in range(N_NEAR):
            owner = (near ^ k) * N_NEAR + (far + n_far - j) % n_far
            span = pl.ds(pl.multiple_of(owner * rows, rows), rows)
            block = query_refs[j][k * rows : (k + 1) * rows, :]
            plain, rope = block[:, :latent], block[:, latent:]
            zero = jnp.zeros_like(rope)
            side_ref[0, span, :latent] = plain
            side_ref[0, span, latent:] = jnp.where(low, rope, zero)
            side_ref[1, span, :LANES] = jnp.where(low, zero, rope)
            side_ref[1, span, LANES:] = plain


def pair_kernel(w_ref, out_ref):
    width = w_ref.shape[2]
    for h in range(w_ref.shape[0]):
        out_ref[h // 2, :, h % 2 * width : (h % 2 + 1) * width] = w_ref[h]


def attend_kernel(scale2, bias_ref, side_ref, cache_ref, out_ref, score_ref, weight_ref):
    n_seq = out_ref.shape[0]
    rows = side_ref.shape[1] // n_seq
    latent = (cache_ref.shape[1] - LANES) // 2
    chunks = latent // LANES
    lane = lax.broadcasted_iota(jnp.int32, (rows, LANES), 1)
    base = PARTS * (lax.broadcasted_iota(jnp.int32, (rows, LANES), 0) // FOLD)
    for h in range(2):
        score_ref[h] = lax.dot_general(
            side_ref[h], cache_ref[:, h * latent : (h + 1) * latent + LANES], NT,
            preferred_element_type=jnp.float32,
        )
    for b in range(n_seq):
        block = slice(b * rows, (b + 1) * rows)
        scores = [score_ref[h, block] + bias_ref[h : h + 1, :] for h in range(2)]
        best = jnp.max(jnp.maximum(*scores), axis=1, keepdims=True)
        best_parts = split_bf16(best, 2)
        best = best_parts[0] + best_parts[1]
        weights = [jnp.exp2((one - best) * scale2) for one in scores]
        for h in range(2):
            weight_ref[h, block] = weights[h].astype(jnp.bfloat16)
        weight_sum = jnp.sum(weights[0] + weights[1], axis=1, keepdims=True)
        stats = jnp.zeros((rows, LANES), jnp.float32)
        for j, part in enumerate(best_parts + split_bf16(weight_sum, 2)):
            stats = jnp.where(lane == base + j, part, stats)
        stats = sum(stats[i * FOLD : (i + 1) * FOLD] for i in range(rows // FOLD))
        out_ref[b, chunks * rows :, :] = stats.astype(jnp.bfloat16)
    value = jnp.dot(weight_ref[0], cache_ref[:, :latent], preferred_element_type=jnp.float32)
    value += jnp.dot(
        weight_ref[1], cache_ref[:, latent + LANES :], preferred_element_type=jnp.float32
    )
    value = value.astype(jnp.bfloat16)
    for b in range(n_seq):
        for c in range(chunks):
            out_ref[b, c * rows : (c + 1) * rows, :] = (
                value[b * rows : (b + 1) * rows, c * LANES : (c + 1) * LANES]
            )


def fresh_kernel(scale2, query_ref, new_ref, best_ref, sum_ref, value_ref):
    rows, width = query_ref.shape[1:]
    latent = width - LANES
    count = new_ref.shape[0] // 2
    heads = rows // count
    token = lax.broadcasted_iota(jnp.int32, (rows, count), 0) // heads
    causal = lax.broadcasted_iota(jnp.int32, (rows, count), 1) <= token
    for r in range(2):
        part = slice(r * rows, (r + 1) * rows)
        mine = new_ref[...].astype(jnp.float32)[r * count : (r + 1) * count]
        new_lat, rope = mine[:, :latent], mine[:, latent:]
        keys = jnp.concatenate([mine, jnp.zeros_like(rope)], axis=1).astype(jnp.bfloat16)
        scores = lax.dot_general(query_ref[r], keys, NT, preferred_element_type=jnp.float32)
        scores = jnp.where(causal, scores * scale2, FILL_LOW)
        best = jnp.max(scores, axis=1, keepdims=True)
        weights = jnp.exp2(scores - best)
        best_ref[part] = jnp.broadcast_to(best, (rows, LANES))
        sum_ref[part] = jnp.broadcast_to(jnp.sum(weights, axis=1, keepdims=True), (rows, LANES))
        weights = weights.astype(jnp.bfloat16).astype(jnp.float32)
        value = weights[:, :1] * new_lat[:1]
        for j in range(1, count):
            value = value + weights[:, j : j + 1] * new_lat[j : j + 1]
        value_ref[part] = value


def merge_kernel(scale2, got_ref, best_ref, sum_ref, value_ref, w_ref, out_ref):
    n_seq = got_ref.shape[0]
    heads, latent = 2 * w_ref.shape[0], w_ref.shape[1]
    rows = best_ref.shape[0] // 2
    chunks = latent // LANES
    tail = chunks * rows
    lane = lax.broadcasted_iota(jnp.int32, (rows, LANES), 1)
    base = PARTS * (lax.broadcasted_iota(jnp.int32, (rows, LANES), 0) // FOLD)
    in_best = (lane >= base) & (lane < base + 2)
    in_sum = (lane >= base + 2) & (lane < base + 4)
    latent_out = []
    for r in range(2):
        part = slice(r * rows, (r + 1) * rows)
        sources = [i for i in range(n_seq) if i // N_NEAR % 2 == r]
        bests, sums = [], []
        for i in sources:
            stats = got_ref[i, tail:, :].astype(jnp.float32)
            stats = jnp.concatenate([stats] * (rows // FOLD), axis=0)
            best = jnp.sum(jnp.where(in_best, stats, 0.0), axis=1, keepdims=True)
            bests.append(best * scale2)
            sums.append(jnp.sum(jnp.where(in_sum, stats, 0.0), axis=1, keepdims=True))
        fresh_best = best_ref[part]
        best = fresh_best
        for one in bests:
            best = jnp.maximum(best, one)
        fresh_factor = jnp.exp2(fresh_best - best)
        factors = [jnp.exp2(one - best) for one in bests]
        total = fresh_factor * sum_ref[part]
        for factor, one in zip(factors, sums):
            total = total + factor * one
        inverse = 1.0 / total
        pieces = []
        for c in range(chunks):
            value = fresh_factor * value_ref[part, c * LANES : (c + 1) * LANES]
            for factor, i in zip(factors, sources):
                value = value + factor * got_ref[i, c * rows : (c + 1) * rows].astype(jnp.float32)
            pieces.append((value * inverse).astype(jnp.bfloat16))
        latent_out.append(jnp.concatenate(pieces, axis=1))
    latent_out = jnp.concatenate(latent_out, axis=0)
    head_of = lax.broadcasted_iota(jnp.int32, out_ref.shape, 0) % heads
    result = jnp.zeros(out_ref.shape, jnp.float32)
    width = out_ref.shape[1]
    for p in range(heads // 2):
        both = jnp.dot(latent_out, w_ref[p], preferred_element_type=jnp.float32)
        result = jnp.where(head_of == 2 * p, both[:, :width], result)
        result = jnp.where(head_of == 2 * p + 1, both[:, width:], result)
    out_ref[...] = result.astype(jnp.bfloat16)


def per_device(latent_pool, block_table, lengths, row_request, queries, new_latent, w_uk, w_uv):
    n_seq = lax.axis_size("seq")
    n_row = lax.axis_size("row")
    group = lax.axis_index("grp")
    _, rows_dev, n_new, head_dev, query_width = queries.shape
    _, page_rows, lat_width = latent_pool.shape[1:]
    latent_dim = w_uk.shape[2]
    value_dim = w_uv.shape[2]
    half_rows = n_new * head_dev
    block_rows = rows_dev * half_rows
    keys = n_row * page_rows
    scale2 = query_width ** (-0.5) * LOG2_E
    swap = [(0, 1), (1, 0)]
    bf16 = jnp.bfloat16

    pool = lax.ppermute(latent_pool[0], "grp", swap)
    table = lax.ppermute(block_table.reshape(1, -1), "grp", swap)
    order = jnp.clip(row_request, 0, row_request.shape[1] - 1)
    packed_shape = (2 * n_row, page_rows // 2, 2 * latent_dim + LANES)
    packed = pl.pallas_call(
        pack_kernel,
        out_shape=jax.ShapeDtypeStruct(packed_shape, bf16),
        in_specs=[smem(), smem(), vmem()],
        out_specs=vmem(),
        compiler_params=params(8),
        name="pack",
    )(order, table, pool)
    pairs = [
        [(base + pair * N_NEAR) * n_row + row for pair in range(2) for row in range(n_row)]
        for base in range(n_seq)
        if base // N_NEAR % 2 == 0
    ]
    got_cache = lax.all_to_all(
        packed, ("seq", "row"), 0, 0, axis_index_groups=pairs, tiled=True
    )

    place = jnp.stack([1 - group, lax.axis_index("seq"), lax.axis_index("row")]).astype(jnp.int32)
    own_query, bias = pl.pallas_call(
        query_kernel,
        out_shape=(
            jax.ShapeDtypeStruct((rows_dev, half_rows, latent_dim + LANES), bf16),
            jax.ShapeDtypeStruct((2, keys), jnp.float32),
        ),
        in_specs=[smem()] * 3 + [vmem()] * 2,
        out_specs=(vmem(), vmem()),
        compiler_params=params(16),
        name="query",
    )(place, lengths, row_request, queries.reshape(block_rows, query_width), w_uk)
    pair = lax.axis_index("seq") // N_NEAR % 2
    same, other = (
        lax.dynamic_index_in_dim(own_query, one, 0, keepdims=False) for one in (pair, 1 - pair)
    )
    near = [same]
    for k in range(1, N_NEAR):
        route = [(s, s ^ (k * N_NEAR)) for s in range(n_seq)]
        near.append(lax.ppermute(other if k % 2 else same, "seq", route))
    near_query = jnp.concatenate(near, axis=0)
    all_query = [near_query]
    for j in range(1, n_seq // N_NEAR):
        route = [(s, s // N_NEAR * N_NEAR + (s + j) % N_NEAR) for s in range(n_seq)]
        all_query.append(lax.ppermute(near_query, "seq", route))

    fresh = pl.pallas_call(
        functools.partial(fresh_kernel, scale2),
        out_shape=[
            jax.ShapeDtypeStruct((block_rows, width), jnp.float32)
            for width in (LANES, LANES, latent_dim)
        ],
        in_specs=[vmem()] * 2,
        out_specs=[vmem()] * 3,
        compiler_params=params(16),
        name="fresh",
    )(own_query, new_latent.reshape(rows_dev * n_new, lat_width))
    sides = pl.pallas_call(
        side_kernel,
        out_shape=jax.ShapeDtypeStruct((2, n_seq * half_rows, latent_dim + LANES), bf16),
        in_specs=[vmem()] * len(all_query),
        out_specs=vmem(),
        compiler_params=params(16),
        name="sides",
    )(*all_query)
    w_pairs = pl.pallas_call(
        pair_kernel,
        out_shape=jax.ShapeDtypeStruct((head_dev // 2, latent_dim, 2 * value_dim), bf16),
        in_specs=[vmem()],
        out_specs=vmem(),
        compiler_params=params(16),
        name="pairs",
    )(w_uv)
    sides, fresh, w_pairs = lax.optimization_barrier((sides, fresh, w_pairs))

    send_shape = (n_seq, half_rows * latent_dim // LANES + FOLD, LANES)
    message = pl.pallas_call(
        functools.partial(attend_kernel, scale2),
        out_shape=jax.ShapeDtypeStruct(send_shape, bf16),
        in_specs=[vmem()] * 3,
        out_specs=vmem(),
        scratch_shapes=[
            pltpu.VMEM((2, n_seq * half_rows, keys), jnp.float32),
            pltpu.VMEM((2, n_seq * half_rows, keys), bf16),
        ],
        compiler_params=params(32),
        name="attend",
    )(bias, sides, got_cache.reshape(keys, -1))
    got = lax.all_to_all(message, "seq", 0, 0, tiled=True)

    result = pl.pallas_call(
        functools.partial(merge_kernel, scale2),
        out_shape=jax.ShapeDtypeStruct((block_rows, value_dim), bf16),
        in_specs=[vmem()] * 5,
        out_specs=vmem(),
        compiler_params=params(16),
        name="merge",
    )(got, *fresh, w_pairs)
    return result.reshape(1, rows_dev, n_new, head_dev, value_dim)


def solution(mesh):
    placed = (
        P("grp", ("seq", "row"), None, None),
        P("grp", ("seq", "row"), None, None),
        P(),
        P("grp", None),
        P("grp", "row", None, "seq", None),
        P("grp", "row", None, None),
        P("seq", None, None),
        P("seq", None, None),
    )
    return jax.shard_map(
        per_device,
        mesh=mesh,
        in_specs=placed,
        out_specs=P("grp", "row", None, "seq", None),
        check_vma=False,
    )
```
